32 devices in a mesh: group: 1, node: 8 (over y, x, core), local: 4 (over z).
Axes of the slice: x: 2, y: 2, z: 4, core: 2. Of those that a mesh axis runs over, the one named last changes fastest.
Arguments:
- queries: bfloat16 [256, 64, 128], P(('group', 'node', 'local')), may hold values from -5 to 5
- key_cache: bfloat16 [256, 4, 96, 128], P(('group', 'node', 'local')), may hold values from -5 to 5
- value_cache: bfloat16 [256, 4, 96, 128], P(('group', 'node', 'local')), may hold values from -15 to 15
- fresh_token_keys: bfloat16 [256, 4, 128], P(('group', 'node', 'local')), may hold values from -5 to 5
- new_values: bfloat16 [256, 4, 128], P(('group', 'node', 'local')), may hold values from -15 to 15
- lengths: int32 [256], P(('group', 'node', 'local')), may hold values from 2 to 96, as said below
- hidden_rows: bfloat16 [256, 4096], P(('group', 'node', 'local')), may hold values from -100 to 100
- norm_gain: bfloat16 [4096], replicated, may hold values from 0.099609375 to 1.8984375
- expert_ids: int32 [256, 8], P(('group', 'node', 'local')), may hold values from 0 to 15, all different within a row; in each aligned block of 8 rows (0 to 7, 8 to 15, ...) at most 8 rows name the same one
- route_scores: float32 [256, 8], P(('group', 'node', 'local')), may hold values from 0.1 to 10
- gate_weight: bfloat16 [32, 4096, 768], P(('node', 'local')), may hold values from -0.09375 to 0.09375
- up_weight: bfloat16 [32, 4096, 768], P(('node', 'local')), may hold values from -0.09375 to 0.09375
- down_weight: bfloat16 [32, 768, 4096], P(('node', 'local')), may hold values from -0.4375 to 0.4375
Outputs:
- context: bfloat16 [256, 8192], P(('group', 'node', 'local'))
- weighted_expert_total: bfloat16 [256, 4096], P(('group', 'node', 'local'))
The draws below stay inside these ranges and needn't reach their ends.
Inputs may be any that keep to these rules, and one draw needn't show every extreme that they name: `expert_ids`: each row names 8 different experts; among the 8 rows of one device no expert is named more than 8 times, and on some device some expert is named exactly 8 times. `lengths`: some request has all 96 slots filled.
All inputs are finite; a program needn't handle non-finite values.
Results may differ from the reference program's by a relative error of at most 0.0065.
Values may be sent and summed in bfloat16 or wider, within the bound.
A program may use at most 128 MiB of HBM per device.

```python
import math
import jax
import jax.numpy as jnp
import numpy as np
from jax import lax

D = 4096
FF = 1536
QH = 64
KVH = 4
HD = 128
TOP = 8
REQ_DEV = 8
CTX = 96
HALF = 768
EXPERTS = 16
MOST = 8
REQS = 256
N_NODE = 8
N_LOCAL = 4


def draw_queries(key, part):
    base_key = jax.random.fold_in(key, 11)
    values = jnp.clip(jax.random.normal(base_key, (REQS, QH, HD), jnp.float32), -4.5, 4.5)
    return values.astype(jnp.bfloat16)


def draw_key_cache(key, part):
    base_key = jax.random.fold_in(key, 13)
    values = jnp.clip(jax.random.normal(base_key, (REQS, KVH, CTX, HD), jnp.float32), -4.5, 4.5)
    return values.astype(jnp.bfloat16)


def draw_lengths(key, part):
    first = jax.random.randint(jax.random.fold_in(key, 21), (REQS,), 2, CTX + 1)
    second = jax.random.randint(jax.random.fold_in(key, 22), (REQS,), 2, CTX + 1)
    chosen = jax.random.randint(jax.random.fold_in(key, 23), (), 0, REQS)
    shorter = jnp.minimum(first, second)
    return jnp.where(jnp.arange(REQS, dtype=jnp.int32) == chosen, CTX, shorter).astype(jnp.int32)


def draw_hidden_rows(key, part):
    base_key = jax.random.fold_in(key, 31)
    row_key = jax.random.fold_in(key, 32)
    column_key = jax.random.fold_in(key, 33)
    column_scale = jnp.exp(jax.random.uniform(column_key, (1, D), jnp.float32, math.log(0.3), math.log(3.0)))
    base = jnp.clip(jax.random.normal(base_key, (REQS, D), jnp.float32), -4.0, 4.0)
    row_scale = jnp.exp(jax.random.uniform(row_key, (REQS, 1), jnp.float32, math.log(0.3), math.log(3.0)))
    return (base * row_scale * column_scale).astype(jnp.bfloat16)


def block_levels(rng, dims, cuts, low, top_value):
    def one(dim, shards_of):
        draws = jax.random.uniform(jax.random.fold_in(jax.random.fold_in(rng, 6), dim), (shards_of,), jnp.float32, low / len(cuts), top_value / len(cuts))
        return jnp.repeat(jnp.exp(draws), dims[dim] // shards_of).reshape((-1,) + (1,) * (len(dims) - dim - 1))

    gain = one(*cuts[0])
    for cut in cuts[1:]:
        gain = gain * one(*cut)
    return gain


def routed_block(rng, own, number, rows, amount, top, reach, slope):
    order = jax.random.permutation(rng, amount)
    heavy_load, usual = load_shares(amount, rows * top, reach, slope, True), load_shares(amount, rows * top, reach, slope, False)
    places = jnp.arange(amount)

    def named(tallies, offset_by):
        used = int((tallies > 0).sum())
        fixed = max(1, used // 4)
        passed = fixed + (places - fixed + offset_by * (used - fixed)) % max(1, amount - fixed)
        return jnp.zeros((amount,), jnp.int32).at[order[jnp.where(places < fixed, places, passed)]].set(jnp.asarray(tallies, jnp.int32))

    tallies = jnp.where(number % 4 == 0, named(heavy_load, number // 4), named(usual, number - number // 4 - 1))
    mixed = jax.random.permutation(jax.random.fold_in(own, 3), amount)
    giver, taker = mixed[0:amount // 2 * 2:2], mixed[1:amount // 2 * 2:2]
    margin = jnp.minimum(tallies[giver] - 1, reach - tallies[taker]) // 2
    margin = jnp.where((giver == order[0]) | (taker == order[0]) | (tallies[taker] == 0), 0, jnp.maximum(margin, 0))
    passed = jax.random.randint(jax.random.fold_in(own, 4), (amount // 2,), 0, 1 << 20) % (margin + 1)
    tallies = tallies.at[giver].add(-passed).at[taker].add(passed)
    members = jnp.searchsorted(jnp.cumsum(tallies), jnp.arange(rows * top), side="right").astype(jnp.int32)
    grid = members.reshape(top, rows).T
    grid = grid[jax.random.permutation(jax.random.fold_in(own, 1), rows)]
    offset_by = jax.random.randint(jax.random.fold_in(own, 2), (rows, 1), 0, top)
    return jnp.take_along_axis(grid, (jnp.arange(top)[None, :] + offset_by) % top, axis=1)


def load_shares(count, total, most, slope, full):
    weights = [(1 << 20) // math.isqrt(rank ** slope) + 1 for rank in range(1, count + 1)]
    largest = most if full else min(most, max(-(-total // count), total * weights[0] // sum(weights)))
    least = 1 if total - largest >= count - 1 else 0
    holding, spare = [largest] + [least] * (count - 1), total - largest - least * (count - 1)
    while spare > 0:
        candidates = [i for i in range(1, count) if holding[i] < largest] or [i for i in range(1, count) if holding[i] < most]
        whole, remaining = sum([weights[i] for i in candidates]), spare
        for i in candidates:
            more = min(most - holding[i], max(1, remaining * weights[i] // whole), spare)
            holding[i] = holding[i] + more
            spare = spare - more
    return np.array(holding)


def scatter_about(rng, dims, scale, reach, split=(), kind=jnp.bfloat16):
    loudness = block_levels(rng, dims, split, -0.22, 0.18) if split else 1.0
    drawn = jax.random.normal(rng, dims, jnp.float32) * scale * loudness
    return jnp.minimum(jnp.maximum(drawn, -reach), reach).astype(kind)


def setup_inputs(seed: int = 0, part: int = 0) -> dict:
    streams_of = jax.random.split(jax.random.key(seed), 14)
    own_keys = jax.random.split(jax.random.fold_in(streams_of[13], part), 14)
    queries = draw_queries(jax.random.fold_in(jax.random.fold_in(streams_of[13], part), 71), part)
    key_cache = draw_key_cache(jax.random.fold_in(jax.random.fold_in(streams_of[13], part), 71), part)
    value_cache = scatter_about(own_keys[2], (REQS, KVH, CTX, HD), 3.0, 15.0, ((0, 32),))
    fresh_token_keys = scatter_about(own_keys[3], (REQS, KVH, HD), 1.0, 5.0, ((0, 32),))
    new_values = scatter_about(own_keys[4], (REQS, KVH, HD), 3.0, 15.0, ((0, 32),))
    lengths = draw_lengths(jax.random.fold_in(jax.random.fold_in(streams_of[13], part), 71), part)
    hidden_rows = draw_hidden_rows(jax.random.fold_in(jax.random.fold_in(streams_of[13], part), 71), part)
    norm_gain = jnp.clip(1.0 + 0.18 * jax.random.normal(streams_of[7], (D,), jnp.float32), 0.099609375, 1.8984375).astype(jnp.bfloat16)
    expert_ids_keys = jax.random.split(jax.random.fold_in(own_keys[8], 1), REQS // REQ_DEV)
    expert_ids_turns = jax.random.permutation(jax.random.fold_in(own_keys[8], 3), REQS // REQ_DEV)
    expert_ids = jax.vmap(lambda own, number: routed_block(jax.random.fold_in(own_keys[8], 2), own, number, REQ_DEV, EXPERTS, TOP, MOST, 2))(expert_ids_keys, expert_ids_turns).reshape((REQS, TOP))
    route_scores = jnp.clip(jnp.exp(math.log(10.0) - 4.6051702 * jax.random.uniform(own_keys[9], (REQS, TOP), jnp.float32) ** block_levels(own_keys[9], (REQS, TOP), ((0, 32),), -0.2, 0.2)), 0.1, 10.0)
    gate_weight = scatter_about(streams_of[10], (2 * EXPERTS, D, HALF), D ** -0.5, 0.09375, ((0, 32),))
    up_weight = scatter_about(streams_of[11], (2 * EXPERTS, D, HALF), D ** -0.5, 0.09375, ((0, 32),))
    down_weight = scatter_about(streams_of[12], (2 * EXPERTS, HALF, D), (FF // 8) ** -0.5, 0.4375, ((0, 32),))
    return dict(queries=queries, key_cache=key_cache, value_cache=value_cache, fresh_token_keys=fresh_token_keys, new_values=new_values, lengths=lengths, hidden_rows=hidden_rows, norm_gain=norm_gain, expert_ids=expert_ids, route_scores=route_scores, gate_weight=gate_weight, up_weight=up_weight, down_weight=down_weight)


def attend_block(queries, key_cache, value_cache, fresh_token_keys, new_values, lengths):
    request_count = queries.shape[0]
    grouped_queries = queries.astype(jnp.float32).reshape(request_count, KVH, QH // KVH, HD)
    keys_f32 = key_cache.astype(jnp.float32)
    values_f32 = value_cache.astype(jnp.float32)
    inverse_scale = 1.0 / math.sqrt(HD)
    scores = jnp.einsum('bkgd,bkpd->bkgp', grouped_queries, keys_f32, precision=lax.Precision.HIGHEST) * inverse_scale
    positions = jnp.arange(CTX, dtype=jnp.int32)
    in_range = positions[None, :] < lengths[:, None]
    scores = jnp.where(in_range[:, None, None, :], scores, -jnp.inf)
    self_token_score = jnp.einsum('uxea,uxa->uxe', grouped_queries, fresh_token_keys.astype(jnp.float32), precision=lax.Precision.HIGHEST) * inverse_scale
    highest = jnp.maximum(lax.optimization_barrier(jnp.max(scores, axis=-1)), self_token_score)
    exponent = jnp.exp(scores - highest[..., None])
    own_exponent = jnp.exp(self_token_score - highest)
    denominator = lax.optimization_barrier(jnp.sum(exponent, axis=-1)) + own_exponent
    probs = lax.optimization_barrier((exponent / denominator[..., None]).astype(jnp.bfloat16)).astype(jnp.float32)
    own_prob = lax.optimization_barrier((own_exponent / denominator).astype(jnp.bfloat16)).astype(jnp.float32)
    mixed = jnp.einsum('bkgp,bkpd->bkgd', probs, values_f32, precision=lax.Precision.HIGHEST)
    mixed = mixed + own_prob[..., None] * new_values.astype(jnp.float32)[:, :, None, :]
    return mixed.reshape(request_count, QH * HD).astype(jnp.bfloat16)

def reference(queries, key_cache, value_cache, fresh_token_keys, new_values, lengths, hidden_rows, norm_gain, expert_ids, route_scores, gate_weight, up_weight, down_weight):
    blocks = REQS // REQ_DEV
    packed = (queries.reshape(blocks, REQ_DEV, QH, HD), key_cache.reshape(blocks, REQ_DEV, KVH, CTX, HD), value_cache.reshape(blocks, REQ_DEV, KVH, CTX, HD), fresh_token_keys.reshape(blocks, REQ_DEV, KVH, HD), new_values.reshape(blocks, REQ_DEV, KVH, HD), lengths.reshape(blocks, REQ_DEV))
    context = lax.map(lambda pieces: attend_block(*pieces), packed).reshape(REQS, QH * HD)
    hidden_f32 = hidden_rows.astype(jnp.float32)
    mean_square = lax.optimization_barrier(jnp.mean(hidden_f32 * hidden_f32, axis=1, keepdims=True))
    normed = (hidden_f32 * lax.rsqrt(mean_square + 1e-06) * norm_gain.astype(jnp.float32)).astype(jnp.bfloat16)
    gates = route_scores / lax.optimization_barrier(jnp.sum(route_scores, axis=1, keepdims=True))
    capacity_all = N_NODE * N_LOCAL * MOST

    def one_expert(total, expert_index):
        chosen = expert_ids == expert_index
        weighting = lax.optimization_barrier(jnp.sum(jnp.where(chosen, gates, 0.0), axis=1))
        reached_mask = jnp.any(chosen, axis=1)
        picked = jnp.nonzero(reached_mask, size=capacity_all, fill_value=0)[0].astype(jnp.int32)
        reached_count = jnp.sum(reached_mask.astype(jnp.int32))
        live = jnp.arange(capacity_all, dtype=jnp.int32) < reached_count
        gate_pair = lax.dynamic_slice_in_dim(gate_weight, 2 * expert_index, 2, 0)
        up_pair = lax.dynamic_slice_in_dim(up_weight, 2 * expert_index, 2, 0)
        down_pair = lax.dynamic_slice_in_dim(down_weight, 2 * expert_index, 2, 0)
        gate_full = jnp.concatenate([gate_pair[0], gate_pair[1]], axis=1)
        up_full = jnp.concatenate([up_pair[0], up_pair[1]], axis=1)
        down_full = down_pair.reshape(2 * HALF, D)
        selected = normed[picked]
        gate_proj = jnp.dot(selected, gate_full, preferred_element_type=jnp.float32)
        up_proj = jnp.dot(selected, up_full, preferred_element_type=jnp.float32)
        activated = (jax.nn.silu(gate_proj) * up_proj).astype(jnp.bfloat16)
        produced = jnp.dot(activated, down_full, preferred_element_type=jnp.float32)
        scaled = jnp.where(live[:, None], weighting[picked][:, None] * produced, 0.0)
        return (total.at[picked].add(scaled), None)
    total, unused = lax.scan(one_expert, jnp.zeros((REQS, D), jnp.float32), jnp.arange(EXPERTS, dtype=jnp.int32))
    return (context, total.astype(jnp.bfloat16))
```

```python
import math

import jax
import jax.numpy as jnp
from jax import lax
from jax.sharding import PartitionSpec as P


def attend(queries, key_cache, value_cache, fresh_token_keys, new_values, lengths):
    request_count, head_count, head_width = queries.shape
    kv_heads = key_cache.shape[1]
    slot_count = key_cache.shape[2]
    grouped_queries = queries.reshape(request_count, kv_heads, head_count // kv_heads, head_width)
    inverse_scale = 1.0 / math.sqrt(head_width)
    scores = (
        jnp.einsum(
            "bkgd,bkpd->bkgp", grouped_queries, key_cache, preferred_element_type=jnp.float32
        )
        * inverse_scale
    )
    positions = jnp.arange(slot_count, dtype=jnp.int32)
    in_range = positions[None, :] < lengths[:, None]
    scores = jnp.where(in_range[:, None, None, :], scores, -jnp.inf)
    self_token_score = (
        jnp.einsum(
            "uxea,uxa->uxe", grouped_queries, fresh_token_keys, preferred_element_type=jnp.float32
        )
        * inverse_scale
    )
    highest = jnp.maximum(jnp.max(scores, axis=-1), self_token_score)
    exponent = jnp.exp(scores - highest[..., None])
    own_exponent = jnp.exp(self_token_score - highest)
    denominator = jnp.sum(exponent, axis=-1) + own_exponent
    probs = (exponent / denominator[..., None]).astype(jnp.bfloat16)
    own_prob = (own_exponent / denominator).astype(jnp.bfloat16)
    mixed = jnp.einsum("bkgp,bkpd->bkgd", probs, value_cache, preferred_element_type=jnp.float32)
    mixed = (
        mixed
        + own_prob.astype(jnp.float32)[..., None] * new_values.astype(jnp.float32)[:, :, None, :]
    )
    return mixed.reshape(request_count, head_count * head_width).astype(jnp.bfloat16)


def routed_expert_rows(arrived, gate_piece, up_piece, down_piece):
    flattened_tokens = arrived.reshape(-1, arrived.shape[-1])
    gate_proj = jnp.dot(flattened_tokens, gate_piece, preferred_element_type=jnp.float32)
    up_proj = jnp.dot(flattened_tokens, up_piece, preferred_element_type=jnp.float32)
    activated = (jax.nn.silu(gate_proj) * up_proj).astype(jnp.bfloat16)
    return jnp.dot(activated, down_piece, preferred_element_type=jnp.float32)


def per_device(
    queries,
    key_cache,
    value_cache,
    fresh_token_keys,
    new_values,
    lengths,
    hidden_rows,
    norm_gain,
    expert_ids,
    route_scores,
    gate_weight,
    up_weight,
    down_weight,
):
    context = attend(queries, key_cache, value_cache, fresh_token_keys, new_values, lengths)
    row_count, model_width = hidden_rows.shape
    axes = ("node", "local")
    devices = lax.axis_size("node") * lax.axis_size("local")
    experts = devices // 2
    hidden_f32 = hidden_rows.astype(jnp.float32)
    mean_square = jnp.mean(hidden_f32 * hidden_f32, axis=1, keepdims=True)
    normed = (hidden_f32 * lax.rsqrt(mean_square + 1e-06) * norm_gain.astype(jnp.float32)).astype(
        jnp.bfloat16
    )
    gates = route_scores / jnp.sum(route_scores, axis=1, keepdims=True)
    matches = expert_ids[:, :, None] == jnp.arange(experts, dtype=jnp.int32)[None, None, :]
    dense_gates = jnp.sum(jnp.where(matches, gates[:, :, None], 0.0), axis=1)
    tokens = lax.all_gather(normed, axes, axis=0, tiled=True)
    all_gates = lax.all_gather(dense_gates, axes, axis=0, tiled=True)
    mine = (lax.axis_index("node") * lax.axis_size("local") + lax.axis_index("local")) // 2
    column = jnp.sum(
        jnp.where(jnp.arange(experts, dtype=jnp.int32)[None, :] == mine, all_gates, 0.0),
        axis=1,
        keepdims=True,
    )
    produced = routed_expert_rows(tokens, gate_weight[0], up_weight[0], down_weight[0])
    weighted = (produced * column).astype(jnp.bfloat16)
    returned = lax.all_to_all(
        weighted.reshape(devices, row_count, model_width), axes, split_axis=0, concat_axis=0, tiled=True
    )
    weighted_expert_total = jnp.sum(returned.astype(jnp.float32), axis=0).astype(jnp.bfloat16)
    return (context, weighted_expert_total)


def solution(mesh):
    placed = (
        P(("group", "node", "local"), None, None),
        P(("group", "node", "local"), None, None, None),
        P(("group", "node", "local"), None, None, None),
        P(("group", "node", "local"), None, None),
        P(("group", "node", "local"), None, None),
        P(("group", "node", "local")),
        P(("group", "node", "local"), None),
        P(),
        P(("group", "node", "local"), None),
        P(("group", "node", "local"), None),
        P(("node", "local"), None, None),
        P(("node", "local"), None, None),
        P(("node", "local"), None, None),
    )
    return jax.shard_map(
        per_device,
        mesh=mesh,
        in_specs=placed,
        out_specs=(P(("group", "node", "local"), None), P(("group", "node", "local"), None)),
        check_vma=False,
    )
```

```python
import functools
import math

import jax
import jax.numpy as jnp
from jax import lax
from jax.experimental import pallas as pl
from jax.experimental.pallas import tpu as pltpu
from jax.sharding import PartitionSpec as P


def attend(queries, key_cache, value_cache, fresh_token_keys, new_values, lengths):
    request_count, head_count, head_width = queries.shape
    kv_heads = key_cache.shape[1]
    slot_count = key_cache.shape[2]
    grouped_queries = queries.reshape(request_count, kv_heads, head_count // kv_heads, head_width)
    inverse_scale = 1.0 / math.sqrt(head_width)
    scores = (
        jnp.einsum(
            "bkgd,bkpd->bkgp", grouped_queries, key_cache, preferred_element_type=jnp.float32
        )
        * inverse_scale
    )
    positions = jnp.arange(slot_count, dtype=jnp.int32)
    in_range = positions[None, :] < lengths[:, None]
    scores = jnp.where(in_range[:, None, None, :], scores, -jnp.inf)
    self_token_score = (
        jnp.einsum(
            "uxea,uxa->uxe", grouped_queries, fresh_token_keys, preferred_element_type=jnp.float32
        )
        * inverse_scale
    )
    highest = jnp.maximum(jnp.max(scores, axis=-1), self_token_score)
    exponent = jnp.exp(scores - highest[..., None])
    own_exponent = jnp.exp(self_token_score - highest)
    denominator = jnp.sum(exponent, axis=-1) + own_exponent
    probs = (exponent / denominator[..., None]).astype(jnp.bfloat16)
    own_prob = (own_exponent / denominator).astype(jnp.bfloat16)
    mixed = jnp.einsum("bkgp,bkpd->bkgd", probs, value_cache, preferred_element_type=jnp.float32)
    mixed = (
        mixed
        + own_prob.astype(jnp.float32)[..., None] * new_values.astype(jnp.float32)[:, :, None, :]
    )
    return mixed.reshape(request_count, head_count * head_width).astype(jnp.bfloat16)


def exchange_orders(node_count, local_count):
    local_bits = [("local", 1 << b) for b in reversed(range(local_count.bit_length() - 1))]
    node_bits = [("node", 1 << b) for b in reversed(range(1, node_count.bit_length() - 1))]
    core = [("node", 1)]
    weights = {bit: 1 << k for k, bit in enumerate(local_bits + node_bits + core)}
    return weights, (local_bits + node_bits + core, local_bits + node_bits[::-1] + core)


def runs_of(slots):
    runs = []
    for slot in sorted(slots):
        if runs and runs[-1][0] + runs[-1][1] == slot:
            runs[-1][1] += 1
        else:
            runs.append([slot, 1])
    return runs


def gather_plan(weights, order):
    held, stages = [0], []
    for bit in order:
        stages.append((bit, runs_of(held)))
        held = held + [slot + weights[bit] for slot in held]
    return stages


def expert_kernel(
    node_count, local_count,
    hidden_ref, gain_ref, ids_ref, scores_ref, gate_hbm, up_hbm, down_hbm,
    out_ref,
    first_rows, second_rows, first_back, second_back, total, tokens, act, gate_w, up_w, down_w,
    weight_sem, send_sem, recv_sem,
):
    width = hidden_ref.shape[1]
    half, quarter = width // 2, width // 4
    count = node_count * local_count
    weights, orders = exchange_orders(node_count, local_count)
    plans = [gather_plan(weights, order) for order in orders]
    rows = (first_rows, second_rows)
    backs = (first_back, second_back)
    place = {"node": lax.axis_index("node"), "local": lax.axis_index("local")}

    def partner(bit):
        axis, step = bit
        return {axis: place[axis] + step - 2 * step * ((place[axis] // step) % 2)}

    loads = [
        pltpu.make_async_copy(source.at[0], target, weight_sem.at[k])
        for k, (source, target) in enumerate(
            ((gate_hbm, gate_w), (up_hbm, up_w), (down_hbm, down_w))
        )
    ]
    for load in loads:
        load.start()
    barrier = pltpu.get_barrier_semaphore()
    for bit in weights:
        pl.semaphore_signal(
            barrier, inc=1, device_id=partner(bit), device_id_type=pl.DeviceIdType.MESH
        )

    hidden = hidden_ref[...].astype(jnp.float32)
    mean_square = jnp.mean(hidden * hidden, axis=1, keepdims=True)
    normed = hidden * lax.rsqrt(mean_square + 1e-06) * gain_ref[...].astype(jnp.float32)
    scores = scores_ref[...]
    gates = scores / jnp.sum(scores, axis=1, keepdims=True)
    lanes = lax.broadcasted_iota(jnp.int32, (8, 128), 1)
    dense = jnp.zeros((8, 128), jnp.float32)
    for j in range(ids_ref.shape[1]):
        dense = dense + jnp.where(lanes == ids_ref[:, j : j + 1], gates[:, j : j + 1], 0.0)
    high = dense.astype(jnp.bfloat16).astype(jnp.float32)
    for q in range(2):
        pair = [normed[:, (2 * q + k) * quarter : (2 * q + k + 1) * quarter] for k in range(2)]
        rows[q][0, :, :quarter] = jnp.concatenate(pair, axis=0).astype(jnp.bfloat16)
    first_rows[0, :, quarter:] = jnp.concatenate([high, dense - high], axis=0).astype(jnp.bfloat16)
    pl.semaphore_wait(barrier, len(weights))

    used = 0
    pending = []
    for stage in range(len(weights)):
        arriving = []
        for q in range(2):
            bit, runs = plans[q][stage]
            for start, size in runs:
                copy = pltpu.make_async_remote_copy(
                    src_ref=rows[q].at[pl.ds(start, size)],
                    dst_ref=rows[q].at[pl.ds(start + weights[bit], size)],
                    send_sem=send_sem.at[used],
                    recv_sem=recv_sem.at[used],
                    device_id=partner(bit),
                    device_id_type=pl.DeviceIdType.MESH,
                )
                copy.start()
                arriving.append(copy)
                used += 1
        for copy in arriving:
            copy.wait_recv()
        pending += arriving
    for copy in pending:
        copy.wait_send()
    for load in loads:
        load.wait()

    tile = tokens.shape[0]
    blocks = tile // 8
    ff = gate_w.shape[1]
    mine = (place["node"] * local_count + place["local"]) // 2

    @pl.loop(0, count // blocks)
    def _(step):
        at = step * blocks
        for q in range(2):
            @pl.loop(0, blocks)
            def _(b):
                both = rows[q][at + b, :, :quarter].astype(jnp.float32)
                into = pl.ds(pl.multiple_of(b * 8, 8), 8)
                for k in range(2):
                    columns = slice((2 * q + k) * quarter, (2 * q + k + 1) * quarter)
                    tokens[into, columns] = both[8 * k : 8 * k + 8]
        split = first_rows[pl.ds(at, blocks), :, quarter:].astype(jnp.float32)
        every = (split[:, :8] + split[:, 8:]).reshape(tile, 128)
        lane = lax.broadcasted_iota(jnp.int32, (tile, 128), 1)
        gate = jnp.sum(jnp.where(lane == mine, every, 0.0), axis=1, keepdims=True)

        @pl.loop(0, ff // 256)
        def _(f):
            columns = pl.ds(pl.multiple_of(f * 256, 256), 256)
            x = tokens[...].astype(jnp.bfloat16)
            g = jnp.dot(x, gate_w[:, columns], preferred_element_type=jnp.float32)
            u = jnp.dot(x, up_w[:, columns], preferred_element_type=jnp.float32)
            act[:, columns] = (g / (1.0 + jnp.exp(-g)) * u).astype(jnp.bfloat16)

        @pl.loop(0, width // 512)
        def _(c):
            columns = pl.ds(pl.multiple_of(c * 512, 512), 512)
            made = jnp.dot(act[...], down_w[:, columns], preferred_element_type=jnp.float32)
            total[pl.ds(at, blocks), :, columns] = (made * gate).reshape(blocks, 8, 512)

    pending = []
    for stage in reversed(range(len(weights))):
        arriving = []
        for q in range(2):
            bit, runs = plans[q][stage]
            weight = weights[bit]
            for start, size in runs:
                @pl.loop(start + weight, start + weight + size)
                def _(p):
                    pair = [
                        total[p, :, (2 * q + k) * quarter : (2 * q + k + 1) * quarter]
                        for k in range(2)
                    ]
                    rows[q][p, :, :quarter] = jnp.concatenate(pair, axis=0).astype(jnp.bfloat16)

                span = pl.ds(start + weight, size)
                copy = pltpu.make_async_remote_copy(
                    src_ref=rows[q].at[span, :, pl.ds(0, quarter)],
                    dst_ref=backs[q].at[span],
                    send_sem=send_sem.at[used],
                    recv_sem=recv_sem.at[used],
                    device_id=partner(bit),
                    device_id_type=pl.DeviceIdType.MESH,
                )
                copy.start()
                arriving.append((q, start, size, weight, copy))
                used += 1
        for q, start, size, weight, copy in arriving:
            copy.wait_recv()

            @pl.loop(start, start + size)
            def _(p):
                both = backs[q][p + weight].astype(jnp.float32)
                for k in range(2):
                    columns = slice((2 * q + k) * quarter, (2 * q + k + 1) * quarter)
                    total[p, :, columns] += both[8 * k : 8 * k + 8]
            pending.append(copy)
    out_ref[...] = total[0].astype(out_ref.dtype)
    for copy in pending:
        copy.wait_send()


def routed_experts(
    hidden_rows, norm_gain, expert_ids, route_scores, gate_weight, up_weight, down_weight
):
    row_count, width = hidden_rows.shape
    node_count = lax.axis_size("node")
    local_count = lax.axis_size("local")
    count = node_count * local_count
    quarter = width // 4
    ff = gate_weight.shape[2]
    weights, orders = exchange_orders(node_count, local_count)
    copies = sum(len(runs) for order in orders for _, runs in gather_plan(weights, order))
    tile = min(256, count * row_count)
    vmem = pl.BlockSpec(memory_space=pltpu.VMEM)
    anywhere = pl.BlockSpec(memory_space=pl.ANY)
    rows = count * row_count
    return pl.pallas_call(
        functools.partial(expert_kernel, node_count, local_count),
        out_shape=jax.ShapeDtypeStruct((row_count, width), jnp.bfloat16),
        in_specs=[vmem] * 4 + [anywhere] * 3,
        out_specs=vmem,
        scratch_shapes=[
            pltpu.VMEM((count, 16, quarter + 128), jnp.bfloat16),
            pltpu.VMEM((count, 16, quarter), jnp.bfloat16),
            pltpu.VMEM((count, 16, quarter), jnp.bfloat16),
            pltpu.VMEM((count, 16, quarter), jnp.bfloat16),
            pltpu.VMEM((count, 8, width), jnp.float32),
            pltpu.VMEM((tile, width), jnp.float32),
            pltpu.VMEM((tile, ff), jnp.bfloat16),
            pltpu.VMEM((width, ff), jnp.bfloat16),
            pltpu.VMEM((width, ff), jnp.bfloat16),
            pltpu.VMEM((ff, width), jnp.bfloat16),
            pltpu.SemaphoreType.DMA((3,)),
            pltpu.SemaphoreType.DMA((2 * copies,)),
            pltpu.SemaphoreType.DMA((2 * copies,)),
        ],
        compiler_params=pltpu.CompilerParams(
            collective_id=0, has_side_effects=True, vmem_limit_bytes=62 * 1024 * 1024
        ),
        cost_estimate=pl.CostEstimate(
            flops=6 * rows * width * ff, bytes_accessed=6 * width * ff, transcendentals=rows * ff
        ),
    )(
        hidden_rows, norm_gain.reshape(1, width), expert_ids, route_scores,
        gate_weight, up_weight, down_weight,
    )


def per_device(
    queries,
    key_cache,
    value_cache,
    fresh_token_keys,
    new_values,
    lengths,
    hidden_rows,
    norm_gain,
    expert_ids,
    route_scores,
    gate_weight,
    up_weight,
    down_weight,
):
    context = attend(queries, key_cache, value_cache, fresh_token_keys, new_values, lengths)
    weighted_expert_total = routed_experts(
        hidden_rows, norm_gain, expert_ids, route_scores, gate_weight, up_weight, down_weight
    )
    return (context, weighted_expert_total)


def solution(mesh):
    placed = (
        P(("group", "node", "local"), None, None),
        P(("group", "node", "local"), None, None, None),
        P(("group", "node", "local"), None, None, None),
        P(("group", "node", "local"), None, None),
        P(("group", "node", "local"), None, None),
        P(("group", "node", "local")),
        P(("group", "node", "local"), None),
        P(),
        P(("group", "node", "local"), None),
        P(("group", "node", "local"), None),
        P(("node", "local"), None, None),
        P(("node", "local"), None, None),
        P(("node", "local"), None, None),
    )
    return jax.shard_map(
        per_device,
        mesh=mesh,
        in_specs=placed,
        out_specs=(P(("group", "node", "local"), None), P(("group", "node", "local"), None)),
        check_vma=False,
    )
```

```python
import functools
import math

import jax
import jax.numpy as jnp
from jax import lax
from jax.experimental import pallas as pl
from jax.experimental.pallas import tpu as pltpu
from jax.sharding import PartitionSpec as P


def attend(queries, key_cache, value_cache, fresh_token_keys, new_values, lengths):
    request_count, head_count, head_width = queries.shape
    kv_heads = key_cache.shape[1]
    slot_count = key_cache.shape[2]
    grouped_queries = queries.reshape(request_count, kv_heads, head_count // kv_heads, head_width)
    inverse_scale = 1.0 / math.sqrt(head_width)
    scores = (
        jnp.einsum(
            "bkgd,bkpd->bkgp", grouped_queries, key_cache, preferred_element_type=jnp.float32
        )
        * inverse_scale
    )
    positions = jnp.arange(slot_count, dtype=jnp.int32)
    in_range = positions[None, :] < lengths[:, None]
    scores = jnp.where(in_range[:, None, None, :], scores, -jnp.inf)
    self_token_score = (
        jnp.einsum(
            "uxea,uxa->uxe", grouped_queries, fresh_token_keys, preferred_element_type=jnp.float32
        )
        * inverse_scale
    )
    highest = jnp.maximum(jnp.max(scores, axis=-1), self_token_score)
    exponent = jnp.exp(scores - highest[..., None])
    own_exponent = jnp.exp(self_token_score - highest)
    denominator = jnp.sum(exponent, axis=-1) + own_exponent
    probs = (exponent / denominator[..., None]).astype(jnp.bfloat16)
    own_prob = (own_exponent / denominator).astype(jnp.bfloat16)
    mixed = jnp.einsum("bkgp,bkpd->bkgd", probs, value_cache, preferred_element_type=jnp.float32)
    mixed = (
        mixed
        + own_prob.astype(jnp.float32)[..., None] * new_values.astype(jnp.float32)[:, :, None, :]
    )
    return mixed.reshape(request_count, head_count * head_width).astype(jnp.bfloat16)


def exchange_orders(node_count, local_count):
    local_bits = [("local", 1 << b) for b in reversed(range(local_count.bit_length() - 1))]
    node_bits = [("node", 1 << b) for b in reversed(range(1, node_count.bit_length() - 1))]
    core = [("node", 1)]
    weights = {bit: 1 << k for k, bit in enumerate(local_bits + node_bits + core)}
    forward = local_bits + node_bits + core
    backward = local_bits + node_bits[::-1] + core
    return weights, (forward, backward, forward, backward)


def runs_of(slots):
    runs = []
    for slot in sorted(slots):
        if runs and runs[-1][0] + runs[-1][1] == slot:
            runs[-1][1] += 1
        else:
            runs.append([slot, 1])
    return runs


def gather_plan(weights, order):
    held, stages = [0], []
    for bit in order:
        stages.append((bit, runs_of(held)))
        held = held + [slot + weights[bit] for slot in held]
    return stages


def expert_kernel(
    node_count, local_count,
    hidden_ref, gain_ref, ids_ref, scores_ref, gate_hbm, up_hbm, down_hbm,
    out_ref, *scratch,
):
    rows, backs = scratch[:4], scratch[4:8]
    total, tokens, act, gate_rows, gate_w, up_w, down_w = scratch[8:15]
    weight_sem, send_sem, recv_sem = scratch[15:]
    width = hidden_ref.shape[1]
    part, piece = width // 4, width // 8
    count = node_count * local_count
    weights, orders = exchange_orders(node_count, local_count)
    plans = [gather_plan(weights, order) for order in orders]
    place = {"node": lax.axis_index("node"), "local": lax.axis_index("local")}

    def partner(bit):
        axis, step = bit
        return {axis: place[axis] + step - 2 * step * ((place[axis] // step) % 2)}

    loads = [
        pltpu.make_async_copy(source.at[0], target, weight_sem.at[k])
        for k, (source, target) in enumerate(
            ((gate_hbm, gate_w), (up_hbm, up_w), (down_hbm, down_w))
        )
    ]
    for load in loads:
        load.start()
    barrier = pltpu.get_barrier_semaphore()
    for bit in weights:
        pl.semaphore_signal(
            barrier, inc=1, device_id=partner(bit), device_id_type=pl.DeviceIdType.MESH
        )

    hidden = hidden_ref[...].astype(jnp.float32)
    mean_square = jnp.mean(hidden * hidden, axis=1, keepdims=True)
    gain = gain_ref[...].astype(jnp.float32)
    gain = jnp.concatenate([gain[k : k + 1] for k in range(width // 128)], axis=1)
    normed = hidden * lax.rsqrt(mean_square + 1e-06) * gain
    scores = scores_ref[...]
    gates = scores / jnp.sum(scores, axis=1, keepdims=True)
    lanes = lax.broadcasted_iota(jnp.int32, (8, 128), 1)
    dense = jnp.zeros((8, 128), jnp.float32)
    for j in range(ids_ref.shape[1]):
        dense = dense + jnp.where(lanes == ids_ref[:, j : j + 1], gates[:, j : j + 1], 0.0)
    high = dense.astype(jnp.bfloat16).astype(jnp.float32)
    for q in range(4):
        pair = [normed[:, q * part + k * piece : q * part + (k + 1) * piece] for k in range(2)]
        rows[q][0, :, :piece] = jnp.concatenate(pair, axis=0).astype(jnp.bfloat16)
    rows[0][0, :, piece:] = jnp.concatenate([high, dense - high], axis=0).astype(jnp.bfloat16)
    pl.semaphore_wait(barrier, len(weights))

    used = 0
    pending = []
    arriving = [[], [], [], []]
    for stage in range(len(weights)):
        for q in range(4):
            for copy in arriving[q]:
                copy.wait_recv()
            arriving[q] = []
            bit, runs = plans[q][stage]
            for start, size in runs:
                copy = pltpu.make_async_remote_copy(
                    src_ref=rows[q].at[pl.ds(start, size)],
                    dst_ref=rows[q].at[pl.ds(start + weights[bit], size)],
                    send_sem=send_sem.at[used],
                    recv_sem=recv_sem.at[used],
                    device_id=partner(bit),
                    device_id_type=pl.DeviceIdType.MESH,
                )
                copy.start()
                arriving[q].append(copy)
                pending.append(copy)
                used += 1

    tile = tokens.shape[0]
    blocks = tile // 8
    ff = gate_w.shape[1]
    mine = (place["node"] * local_count + place["local"]) // 2

    def assemble(q, at):
        @pl.loop(0, blocks // 2)
        def _(b):
            one = rows[q][at + 2 * b, :, :piece].astype(jnp.float32)
            two = rows[q][at + 2 * b + 1, :, :piece].astype(jnp.float32)
            into = pl.ds(pl.multiple_of(b * 16, 16), 16)
            for k in range(2):
                both = jnp.concatenate([one[8 * k : 8 * k + 8], two[8 * k : 8 * k + 8]], axis=0)
                columns = slice(q * part + k * piece, q * part + (k + 1) * piece)
                tokens[into, columns] = both.astype(jnp.bfloat16)

    for q in range(4):
        for copy in arriving[q]:
            copy.wait_recv()
        assemble(q, 0)
    for load in loads:
        load.wait()

    @pl.loop(0, count // blocks)
    def _(step):
        at = step * blocks
        into = pl.ds(pl.multiple_of(step * tile, tile), tile)

        @pl.when(step > 0)
        def _():
            for q in range(4):
                assemble(q, at)

        split = rows[0][pl.ds(at, blocks), :, piece:].astype(jnp.float32)
        every = (split[:, :8] + split[:, 8:]).reshape(tile, 128)
        lane = lax.broadcasted_iota(jnp.int32, (tile, 128), 1)
        gate = jnp.sum(jnp.where(lane == mine, every, 0.0), axis=1, keepdims=True)
        gate_rows[into, :] = jnp.broadcast_to(gate, (tile, 128))

        @pl.loop(0, ff // 256)
        def _(f):
            columns = pl.ds(pl.multiple_of(f * 256, 256), 256)
            g = jnp.dot(tokens[...], gate_w[:, columns], preferred_element_type=jnp.float32)
            u = jnp.dot(tokens[...], up_w[:, columns], preferred_element_type=jnp.float32)
            act[into, columns] = (g / (1.0 + jnp.exp(-g)) * u).astype(jnp.bfloat16)

    for copy in pending:
        copy.wait_send()

    def send_back(q, stage, used):
        bit, runs = plans[q][stage]
        weight = weights[bit]
        started = []
        for start, size in runs:
            @pl.loop(start + weight, start + weight + size)
            def _(p):
                pair = [
                    total[p, :, q * part + k * piece : q * part + (k + 1) * piece]
                    for k in range(2)
                ]
                rows[q][p, :, :piece] = jnp.concatenate(pair, axis=0).astype(jnp.bfloat16)

            span = pl.ds(start + weight, size)
            copy = pltpu.make_async_remote_copy(
                src_ref=rows[q].at[span, :, pl.ds(0, piece)],
                dst_ref=backs[q].at[span],
                send_sem=send_sem.at[used],
                recv_sem=recv_sem.at[used],
                device_id=partner(bit),
                device_id_type=pl.DeviceIdType.MESH,
            )
            copy.start()
            started.append((start, size, weight, copy))
            used += 1
        return started, used

    def take_back(q, started):
        for start, size, weight, copy in started:
            copy.wait_recv()

            @pl.loop(start, start + size)
            def _(p):
                both = backs[q][p + weight].astype(jnp.float32)
                for k in range(2):
                    columns = slice(q * part + k * piece, q * part + (k + 1) * piece)
                    total[p, :, columns] += both[8 * k : 8 * k + 8]

    pending = []
    last = len(weights) - 1
    for stage in reversed(range(len(weights))):
        for q in range(4):
            if stage == last:
                @pl.loop(0, count // blocks)
                def _(step):
                    into = pl.ds(pl.multiple_of(step * tile, tile), tile)
                    for k in range(2):
                        columns = slice(q * part + k * piece, q * part + (k + 1) * piece)
                        made = jnp.dot(
                            act[into, :], down_w[:, columns], preferred_element_type=jnp.float32
                        )
                        made = made * gate_rows[into, :1]
                        total[pl.ds(step * blocks, blocks), :, columns] = made.reshape(
                            blocks, 8, piece
                        )
            else:
                take_back(q, arriving[q])
            arriving[q], used = send_back(q, stage, used)
            pending += [entry[3] for entry in arriving[q]]
    for q in range(4):
        take_back(q, arriving[q])
    out_ref[...] = total[0].astype(out_ref.dtype)
    for copy in pending:
        copy.wait_send()


def routed_experts(
    hidden_rows, norm_gain, expert_ids, route_scores, gate_weight, up_weight, down_weight
):
    row_count, width = hidden_rows.shape
    node_count = lax.axis_size("node")
    local_count = lax.axis_size("local")
    count = node_count * local_count
    piece = width // 8
    ff = gate_weight.shape[2]
    weights, orders = exchange_orders(node_count, local_count)
    copies = sum(len(runs) for order in orders for _, runs in gather_plan(weights, order))
    tile = min(256, count * row_count)
    vmem = pl.BlockSpec(memory_space=pltpu.VMEM)
    anywhere = pl.BlockSpec(memory_space=pl.ANY)
    rows = count * row_count
    return pl.pallas_call(
        functools.partial(expert_kernel, node_count, local_count),
        out_shape=jax.ShapeDtypeStruct((row_count, width), jnp.bfloat16),
        in_specs=[vmem] * 4 + [anywhere] * 3,
        out_specs=vmem,
        scratch_shapes=[
            pltpu.VMEM((count, 16, piece + 128), jnp.bfloat16),
            *[pltpu.VMEM((count, 16, piece), jnp.bfloat16)] * 7,
            pltpu.VMEM((count, 8, width), jnp.float32),
            pltpu.VMEM((tile, width), jnp.bfloat16),
            pltpu.VMEM((rows, ff), jnp.bfloat16),
            pltpu.VMEM((rows, 128), jnp.float32),
            pltpu.VMEM((width, ff), jnp.bfloat16),
            pltpu.VMEM((width, ff), jnp.bfloat16),
            pltpu.VMEM((ff, width), jnp.bfloat16),
            pltpu.SemaphoreType.DMA((3,)),
            pltpu.SemaphoreType.DMA((2 * copies,)),
            pltpu.SemaphoreType.DMA((2 * copies,)),
        ],
        compiler_params=pltpu.CompilerParams(
            collective_id=0, has_side_effects=True, vmem_limit_bytes=62 * 1024 * 1024
        ),
        cost_estimate=pl.CostEstimate(
            flops=6 * rows * width * ff, bytes_accessed=6 * width * ff, transcendentals=rows * ff
        ),
    )(
        hidden_rows, norm_gain.reshape(width // 128, 128), expert_ids, route_scores,
        gate_weight, up_weight, down_weight,
    )


def per_device(
    queries,
    key_cache,
    value_cache,
    fresh_token_keys,
    new_values,
    lengths,
    hidden_rows,
    norm_gain,
    expert_ids,
    route_scores,
    gate_weight,
    up_weight,
    down_weight,
):
    context = attend(queries, key_cache, value_cache, fresh_token_keys, new_values, lengths)
    weighted_expert_total = routed_experts(
        hidden_rows, norm_gain, expert_ids, route_scores, gate_weight, up_weight, down_weight
    )
    return (context, weighted_expert_total)


def solution(mesh):
    placed = (
        P(("group", "node", "local"), None, None),
        P(("group", "node", "local"), None, None, None),
        P(("group", "node", "local"), None, None, None),
        P(("group", "node", "local"), None, None),
        P(("group", "node", "local"), None, None),
        P(("group", "node", "local")),
        P(("group", "node", "local"), None),
        P(),
        P(("group", "node", "local"), None),
        P(("group", "node", "local"), None),
        P(("node", "local"), None, None),
        P(("node", "local"), None, None),
        P(("node", "local"), None, None),
    )
    return jax.shard_map(
        per_device,
        mesh=mesh,
        in_specs=placed,
        out_specs=(P(("group", "node", "local"), None), P(("group", "node", "local"), None)),
        check_vma=False,
    )
```

```python
import functools
import math

import jax
import jax.numpy as jnp
from jax import lax
from jax.experimental import pallas as pl
from jax.experimental.pallas import tpu as pltpu
from jax.sharding import PartitionSpec as P


def attend_request(b, queries, keys, values, fresh_keys, new_values, lengths, context):
    kv_heads, slot_count, head_width = keys.shape[1:]
    group = queries.shape[1] // kv_heads
    inverse_scale = 1.0 / math.sqrt(head_width)
    in_range = lax.broadcasted_iota(jnp.int32, (group, slot_count), 1) < lengths[b]
    fresh = fresh_keys[b].astype(jnp.float32)
    newest = new_values[b].astype(jnp.float32)
    for k in range(kv_heads):
        query = queries[b, k * group : (k + 1) * group]
        scores = lax.dot_general(
            query, keys[b, k], (((1,), (1,)), ((), ())), preferred_element_type=jnp.float32
        )
        scores = jnp.where(in_range, scores * inverse_scale, -jnp.inf)
        own = jnp.sum(query.astype(jnp.float32) * fresh[k : k + 1], axis=1, keepdims=True)
        own = own * inverse_scale
        highest = jnp.maximum(jnp.max(scores, axis=1, keepdims=True), own)
        exponent = jnp.exp(scores - highest)
        own_exponent = jnp.exp(own - highest)
        denominator = jnp.sum(exponent, axis=1, keepdims=True) + own_exponent
        probs = (exponent / denominator).astype(jnp.bfloat16)
        own_prob = (own_exponent / denominator).astype(jnp.bfloat16).astype(jnp.float32)
        mixed = jnp.dot(probs, values[b, k], preferred_element_type=jnp.float32)
        mixed = mixed + own_prob * newest[k : k + 1]
        context[b, k * group : (k + 1) * group] = mixed.astype(jnp.bfloat16)


def exchange_orders(node_count, local_count):
    local_bits = [("local", 1 << b) for b in reversed(range(local_count.bit_length() - 1))]
    node_bits = [("node", 1 << b) for b in reversed(range(1, node_count.bit_length() - 1))]
    core = [("node", 1)]
    weights = {bit: 1 << k for k, bit in enumerate(local_bits + node_bits + core)}
    forward = local_bits + node_bits + core
    backward = local_bits + node_bits[::-1] + core
    return weights, (forward, backward, forward, backward)


def runs_of(slots):
    runs = []
    for slot in sorted(slots):
        if runs and runs[-1][0] + runs[-1][1] == slot:
            runs[-1][1] += 1
        else:
            runs.append([slot, 1])
    return runs


def gather_plan(weights, order):
    held, stages = [0], []
    for bit in order:
        stages.append((bit, runs_of(held)))
        held = held + [slot + weights[bit] for slot in held]
    return stages


def expert_kernel(
    node_count, local_count,
    queries, fresh_keys, new_values, lengths, hidden_ref, gain_ref, ids_ref, scores_ref,
    key_hbm, value_hbm, gate_hbm, up_hbm, down_hbm,
    context, out_ref, *scratch,
):
    rows, backs = scratch[:4], scratch[4:8]
    total, tokens, act, gate_rows, gate_w, up_w, down_w = scratch[8:15]
    keys, values, weight_sem, send_sem, recv_sem = scratch[15:]
    width = hidden_ref.shape[1]
    part, piece = width // 4, width // 8
    count = node_count * local_count
    weights, orders = exchange_orders(node_count, local_count)
    plans = [gather_plan(weights, order) for order in orders]
    place = {"node": lax.axis_index("node"), "local": lax.axis_index("local")}

    def partner(bit):
        axis, step = bit
        return {axis: place[axis] + step - 2 * step * ((place[axis] // step) % 2)}

    loads = [
        pltpu.make_async_copy(source.at[0], target, weight_sem.at[k])
        for k, (source, target) in enumerate(
            ((gate_hbm, gate_w), (up_hbm, up_w), (down_hbm, down_w))
        )
    ]
    caches = [
        pltpu.make_async_copy(key_hbm, keys, weight_sem.at[3]),
        pltpu.make_async_copy(value_hbm, values, weight_sem.at[4]),
    ]
    for load in caches + loads:
        load.start()
    barrier = pltpu.get_barrier_semaphore()
    for bit in weights:
        pl.semaphore_signal(
            barrier, inc=1, device_id=partner(bit), device_id_type=pl.DeviceIdType.MESH
        )

    hidden = hidden_ref[...].astype(jnp.float32)
    mean_square = jnp.mean(hidden * hidden, axis=1, keepdims=True)
    gain = gain_ref[...].astype(jnp.float32)
    gain = jnp.concatenate([gain[k : k + 1] for k in range(width // 128)], axis=1)
    normed = hidden * lax.rsqrt(mean_square + 1e-06) * gain
    scores = scores_ref[...]
    gates = scores / jnp.sum(scores, axis=1, keepdims=True)
    lanes = lax.broadcasted_iota(jnp.int32, (8, 128), 1)
    dense = jnp.zeros((8, 128), jnp.float32)
    for j in range(ids_ref.shape[1]):
        dense = dense + jnp.where(lanes == ids_ref[:, j : j + 1], gates[:, j : j + 1], 0.0)
    high = dense.astype(jnp.bfloat16).astype(jnp.float32)
    for q in range(4):
        pair = [normed[:, q * part + k * piece : q * part + (k + 1) * piece] for k in range(2)]
        rows[q][0, :, :piece] = jnp.concatenate(pair, axis=0).astype(jnp.bfloat16)
    rows[0][0, :, piece:] = jnp.concatenate([high, dense - high], axis=0).astype(jnp.bfloat16)
    pl.semaphore_wait(barrier, len(weights))

    used = 0
    pending = []
    arriving = [[], [], [], []]
    for stage in range(len(weights)):
        for q in range(4):
            for copy in arriving[q]:
                copy.wait_recv()
            arriving[q] = []
            bit, runs = plans[q][stage]
            for start, size in runs:
                copy = pltpu.make_async_remote_copy(
                    src_ref=rows[q].at[pl.ds(start, size)],
                    dst_ref=rows[q].at[pl.ds(start + weights[bit], size)],
                    send_sem=send_sem.at[used],
                    recv_sem=recv_sem.at[used],
                    device_id=partner(bit),
                    device_id_type=pl.DeviceIdType.MESH,
                )
                copy.start()
                arriving[q].append(copy)
                pending.append(copy)
                used += 1
        turn = stage - max(0, len(weights) - 3)
        if turn == 0:
            for load in caches:
                load.wait()
        if turn >= 0:
            requests = queries.shape[0]
            @pl.loop(turn * requests // 3, (turn + 1) * requests // 3)
            def _(b):
                attend_request(
                    b, queries, keys, values, fresh_keys, new_values, lengths, context
                )

    tile = tokens.shape[0]
    blocks = tile // 8
    ff = gate_w.shape[1]
    mine = (place["node"] * local_count + place["local"]) // 2

    def assemble(q, at):
        @pl.loop(0, blocks // 2)
        def _(b):
            one = rows[q][at + 2 * b, :, :piece].astype(jnp.float32)
            two = rows[q][at + 2 * b + 1, :, :piece].astype(jnp.float32)
            into = pl.ds(pl.multiple_of(b * 16, 16), 16)
            for k in range(2):
                both = jnp.concatenate([one[8 * k : 8 * k + 8], two[8 * k : 8 * k + 8]], axis=0)
                columns = slice(q * part + k * piece, q * part + (k + 1) * piece)
                tokens[into, columns] = both.astype(jnp.bfloat16)

    for q in range(4):
        for copy in arriving[q]:
            copy.wait_recv()
        assemble(q, 0)
    for load in loads:
        load.wait()

    @pl.loop(0, count // blocks)
    def _(step):
        at = step * blocks
        into = pl.ds(pl.multiple_of(step * tile, tile), tile)

        @pl.when(step > 0)
        def _():
            for q in range(4):
                assemble(q, at)

        split = rows[0][pl.ds(at, blocks), :, piece:].astype(jnp.float32)
        every = (split[:, :8] + split[:, 8:]).reshape(tile, 128)
        lane = lax.broadcasted_iota(jnp.int32, (tile, 128), 1)
        gate = jnp.sum(jnp.where(lane == mine, every, 0.0), axis=1, keepdims=True)
        gate_rows[into, :] = jnp.broadcast_to(gate, (tile, 128))

        @pl.loop(0, ff // 256)
        def _(f):
            columns = pl.ds(pl.multiple_of(f * 256, 256), 256)
            g = jnp.dot(tokens[...], gate_w[:, columns], preferred_element_type=jnp.float32)
            u = jnp.dot(tokens[...], up_w[:, columns], preferred_element_type=jnp.float32)
            act[into, columns] = (g / (1.0 + jnp.exp(-g)) * u).astype(jnp.bfloat16)

    for copy in pending:
        copy.wait_send()

    def send_back(q, stage, used):
        bit, runs = plans[q][stage]
        weight = weights[bit]
        started = []
        for start, size in runs:
            @pl.loop(start + weight, start + weight + size)
            def _(p):
                pair = [
                    total[p, :, q * part + k * piece : q * part + (k + 1) * piece]
                    for k in range(2)
                ]
                rows[q][p, :, :piece] = jnp.concatenate(pair, axis=0).astype(jnp.bfloat16)

            span = pl.ds(start + weight, size)
            copy = pltpu.make_async_remote_copy(
                src_ref=rows[q].at[span, :, pl.ds(0, piece)],
                dst_ref=backs[q].at[span],
                send_sem=send_sem.at[used],
                recv_sem=recv_sem.at[used],
                device_id=partner(bit),
                device_id_type=pl.DeviceIdType.MESH,
            )
            copy.start()
            started.append((start, size, weight, copy))
            used += 1
        return started, used

    def take_back(q, started):
        for start, size, weight, copy in started:
            copy.wait_recv()

            @pl.loop(start, start + size)
            def _(p):
                both = backs[q][p + weight].astype(jnp.float32)
                for k in range(2):
                    columns = slice(q * part + k * piece, q * part + (k + 1) * piece)
                    total[p, :, columns] += both[8 * k : 8 * k + 8]

    pending = []
    last = len(weights) - 1
    for stage in reversed(range(len(weights))):
        for q in range(4):
            if stage == last:
                @pl.loop(0, count // blocks)
                def _(step):
                    into = pl.ds(pl.multiple_of(step * tile, tile), tile)
                    for k in range(2):
                        columns = slice(q * part + k * piece, q * part + (k + 1) * piece)
                        made = jnp.dot(
                            act[into, :], down_w[:, columns], preferred_element_type=jnp.float32
                        )
                        made = made * gate_rows[into, :1]
                        total[pl.ds(step * blocks, blocks), :, columns] = made.reshape(
                            blocks, 8, piece
                        )
            else:
                take_back(q, arriving[q])
            arriving[q], used = send_back(q, stage, used)
            pending += [entry[3] for entry in arriving[q]]
    for q in range(4):
        take_back(q, arriving[q])
    out_ref[...] = total[0].astype(out_ref.dtype)
    for copy in pending:
        copy.wait_send()


def attention_and_experts(
    queries, key_cache, value_cache, fresh_token_keys, new_values, lengths, hidden_rows, norm_gain, expert_ids, route_scores, gate_weight, up_weight, down_weight
):
    row_count, width = hidden_rows.shape
    node_count = lax.axis_size("node")
    local_count = lax.axis_size("local")
    count = node_count * local_count
    piece = width // 8
    ff = gate_weight.shape[2]
    weights, orders = exchange_orders(node_count, local_count)
    copies = sum(len(runs) for order in orders for _, runs in gather_plan(weights, order))
    tile = min(256, count * row_count)
    vmem = pl.BlockSpec(memory_space=pltpu.VMEM)
    anywhere = pl.BlockSpec(memory_space=pl.ANY)
    rows = count * row_count
    return pl.pallas_call(
        functools.partial(expert_kernel, node_count, local_count),
        out_shape=(
            jax.ShapeDtypeStruct(queries.shape, jnp.bfloat16),
            jax.ShapeDtypeStruct((row_count, width), jnp.bfloat16),
        ),
        in_specs=[vmem] * 3
        + [pl.BlockSpec(memory_space=pltpu.SMEM)]
        + [vmem] * 4
        + [anywhere] * 5,
        out_specs=(vmem, vmem),
        scratch_shapes=[
            pltpu.VMEM((count, 16, piece + 128), jnp.bfloat16),
            *[pltpu.VMEM((count, 16, piece), jnp.bfloat16)] * 7,
            pltpu.VMEM((count, 8, width), jnp.float32),
            pltpu.VMEM((tile, width), jnp.bfloat16),
            pltpu.VMEM((rows, ff), jnp.bfloat16),
            pltpu.VMEM((rows, 128), jnp.float32),
            pltpu.VMEM((width, ff), jnp.bfloat16),
            pltpu.VMEM((width, ff), jnp.bfloat16),
            pltpu.VMEM((ff, width), jnp.bfloat16),
            pltpu.VMEM(key_cache.shape, jnp.bfloat16),
            pltpu.VMEM(value_cache.shape, jnp.bfloat16),
            pltpu.SemaphoreType.DMA((5,)),
            pltpu.SemaphoreType.DMA((2 * copies,)),
            pltpu.SemaphoreType.DMA((2 * copies,)),
        ],
        compiler_params=pltpu.CompilerParams(
            collective_id=0, has_side_effects=True, vmem_limit_bytes=62 * 1024 * 1024
        ),
        cost_estimate=pl.CostEstimate(
            flops=6 * rows * width * ff, bytes_accessed=6 * width * ff, transcendentals=rows * ff
        ),
    )(
        queries, fresh_token_keys, new_values, lengths,
        hidden_rows, norm_gain.reshape(width // 128, 128), expert_ids, route_scores,
        key_cache, value_cache,
        gate_weight, up_weight, down_weight,
    )


def per_device(
    queries,
    key_cache,
    value_cache,
    fresh_token_keys,
    new_values,
    lengths,
    hidden_rows,
    norm_gain,
    expert_ids,
    route_scores,
    gate_weight,
    up_weight,
    down_weight,
):
    context, weighted_expert_total = attention_and_experts(
        queries, key_cache, value_cache, fresh_token_keys, new_values, lengths,
        hidden_rows, norm_gain, expert_ids, route_scores, gate_weight, up_weight, down_weight,
    )
    context = context.reshape(queries.shape[0], queries.shape[1] * queries.shape[2])
    return (context, weighted_expert_total)


def solution(mesh):
    placed = (
        P(("group", "node", "local"), None, None),
        P(("group", "node", "local"), None, None, None),
        P(("group", "node", "local"), None, None, None),
        P(("group", "node", "local"), None, None),
        P(("group", "node", "local"), None, None),
        P(("group", "node", "local")),
        P(("group", "node", "local"), None),
        P(),
        P(("group", "node", "local"), None),
        P(("group", "node", "local"), None),
        P(("node", "local"), None, None),
        P(("node", "local"), None, None),
        P(("node", "local"), None, None),
    )
    return jax.shard_map(
        per_device,
        mesh=mesh,
        in_specs=placed,
        out_specs=(P(("group", "node", "local"), None), P(("group", "node", "local"), None)),
        check_vma=False,
    )
```

```python
import functools
import math

import jax
import jax.numpy as jnp
from jax import lax
from jax.experimental import pallas as pl
from jax.experimental.pallas import tpu as pltpu
from jax.sharding import PartitionSpec as P


def attend_request(b, queries, keys, values, fresh_keys, new_values, lengths, context):
    kv_heads, slot_count, head_width = keys.shape[1:]
    group = queries.shape[1] // kv_heads
    inverse_scale = 1.0 / math.sqrt(head_width)
    in_range = lax.broadcasted_iota(jnp.int32, (group, slot_count), 1) < lengths[b]
    fresh = fresh_keys[b].astype(jnp.float32)
    newest = new_values[b].astype(jnp.float32)
    for k in range(kv_heads):
        query = queries[b, k * group : (k + 1) * group]
        scores = lax.dot_general(
            query, keys[b, k], (((1,), (1,)), ((), ())), preferred_element_type=jnp.float32
        )
        scores = jnp.where(in_range, scores * inverse_scale, -jnp.inf)
        own = jnp.sum(query.astype(jnp.float32) * fresh[k : k + 1], axis=1, keepdims=True)
        own = own * inverse_scale
        highest = jnp.maximum(jnp.max(scores, axis=1, keepdims=True), own)
        exponent = jnp.exp(scores - highest)
        own_exponent = jnp.exp(own - highest)
        denominator = jnp.sum(exponent, axis=1, keepdims=True) + own_exponent
        probs = (exponent / denominator).astype(jnp.bfloat16)
        own_prob = (own_exponent / denominator).astype(jnp.bfloat16).astype(jnp.float32)
        mixed = jnp.dot(probs, values[b, k], preferred_element_type=jnp.float32)
        mixed = mixed + own_prob * newest[k : k + 1]
        context[b, k * group : (k + 1) * group] = mixed.astype(jnp.bfloat16)


def exchange_orders(node_count, local_count):
    local_bits = [("local", 1 << b) for b in reversed(range(local_count.bit_length() - 1))]
    node_bits = [("node", 1 << b) for b in reversed(range(1, node_count.bit_length() - 1))]
    core = [("node", 1)]
    weights = {bit: 1 << k for k, bit in enumerate(local_bits + node_bits + core)}
    forward = local_bits + node_bits + core
    backward = local_bits + node_bits[::-1] + core
    return weights, (forward, backward, forward, backward)


def runs_of(slots):
    runs = []
    for slot in sorted(slots):
        if runs and runs[-1][0] + runs[-1][1] == slot:
            runs[-1][1] += 1
        else:
            runs.append([slot, 1])
    return runs


def gather_plan(weights, order):
    held, stages = [0], []
    for bit in order:
        stages.append((bit, runs_of(held)))
        held = held + [slot + weights[bit] for slot in held]
    return stages


def expert_kernel(
    node_count, local_count,
    queries, fresh_keys, new_values, lengths, hidden_ref, gain_ref, ids_ref, scores_ref,
    key_hbm, value_hbm, gate_hbm, up_hbm, down_hbm,
    context, out_ref, *scratch,
):
    rows, backs = scratch[:4], scratch[4:8]
    total, tokens, act, gate_rows, gate_w, up_w, down_w = scratch[8:15]
    keys, values, weight_sem, send_sem, recv_sem = scratch[15:]
    width = hidden_ref.shape[1]
    part, piece = width // 4, width // 8
    count = node_count * local_count
    weights, orders = exchange_orders(node_count, local_count)
    plans = [gather_plan(weights, order) for order in orders]
    place = {"node": lax.axis_index("node"), "local": lax.axis_index("local")}

    def partner(bit):
        axis, step = bit
        return {axis: place[axis] + step - 2 * step * ((place[axis] // step) % 2)}

    loads = [
        pltpu.make_async_copy(source.at[0], target, weight_sem.at[k])
        for k, (source, target) in enumerate(
            ((gate_hbm, gate_w), (up_hbm, up_w), (down_hbm, down_w))
        )
    ]
    caches = [
        pltpu.make_async_copy(key_hbm, keys, weight_sem.at[3]),
        pltpu.make_async_copy(value_hbm, values, weight_sem.at[4]),
    ]
    for load in caches + loads:
        load.start()
    barrier = pltpu.get_barrier_semaphore()
    for bit in weights:
        pl.semaphore_signal(
            barrier, inc=1, device_id=partner(bit), device_id_type=pl.DeviceIdType.MESH
        )

    hidden = hidden_ref[...].astype(jnp.float32)
    mean_square = jnp.mean(hidden * hidden, axis=1, keepdims=True)
    gain = gain_ref[...].astype(jnp.float32)
    gain = jnp.concatenate([gain[k : k + 1] for k in range(width // 128)], axis=1)
    normed = hidden * lax.rsqrt(mean_square + 1e-06) * gain
    scores = scores_ref[...]
    gates = scores / jnp.sum(scores, axis=1, keepdims=True)
    lanes = lax.broadcasted_iota(jnp.int32, (8, 128), 1)
    dense = jnp.zeros((8, 128), jnp.float32)
    for j in range(ids_ref.shape[1]):
        dense = dense + jnp.where(lanes == ids_ref[:, j : j + 1], gates[:, j : j + 1], 0.0)
    high = dense.astype(jnp.bfloat16).astype(jnp.float32)
    for q in range(4):
        pair = [normed[:, q * part + k * piece : q * part + (k + 1) * piece] for k in range(2)]
        rows[q][0, :, :piece] = jnp.concatenate(pair, axis=0).astype(jnp.bfloat16)
    rows[0][0, :, piece:] = jnp.concatenate([high, dense - high], axis=0).astype(jnp.bfloat16)
    pl.semaphore_wait(barrier, len(weights))

    used = 0
    pending = []
    arriving = [[], [], [], []]
    for stage in range(len(weights)):
        for q in range(4):
            for copy in arriving[q]:
                copy.wait_recv()
            arriving[q] = []
            bit, runs = plans[q][stage]
            for start, size in runs:
                copy = pltpu.make_async_remote_copy(
                    src_ref=rows[q].at[pl.ds(start, size)],
                    dst_ref=rows[q].at[pl.ds(start + weights[bit], size)],
                    send_sem=send_sem.at[used],
                    recv_sem=recv_sem.at[used],
                    device_id=partner(bit),
                    device_id_type=pl.DeviceIdType.MESH,
                )
                copy.start()
                arriving[q].append(copy)
                pending.append(copy)
                used += 1
        turn = stage - max(0, len(weights) - 3)
        if turn == 0:
            for load in caches:
                load.wait()
        if turn >= 0:
            requests = queries.shape[0]
            @pl.loop(turn * requests // 3, (turn + 1) * requests // 3, unroll=True)
            def _(b):
                attend_request(
                    b, queries, keys, values, fresh_keys, new_values, lengths, context
                )

    tile = tokens.shape[0]
    blocks = tile // 8
    ff = gate_w.shape[1]
    mine = (place["node"] * local_count + place["local"]) // 2

    def assemble(q, at):
        @pl.loop(0, blocks // 2)
        def _(b):
            one = rows[q][at + 2 * b, :, :piece].astype(jnp.float32)
            two = rows[q][at + 2 * b + 1, :, :piece].astype(jnp.float32)
            into = pl.ds(pl.multiple_of(b * 16, 16), 16)
            for k in range(2):
                both = jnp.concatenate([one[8 * k : 8 * k + 8], two[8 * k : 8 * k + 8]], axis=0)
                columns = slice(q * part + k * piece, q * part + (k + 1) * piece)
                tokens[into, columns] = both.astype(jnp.bfloat16)

    for q in range(4):
        for copy in arriving[q]:
            copy.wait_recv()
        assemble(q, 0)
    for load in loads:
        load.wait()

    @pl.loop(0, count // blocks)
    def _(step):
        at = step * blocks
        into = pl.ds(pl.multiple_of(step * tile, tile), tile)

        @pl.when(step > 0)
        def _():
            for q in range(4):
                assemble(q, at)

        split = rows[0][pl.ds(at, blocks), :, piece:].astype(jnp.float32)
        every = (split[:, :8] + split[:, 8:]).reshape(tile, 128)
        lane = lax.broadcasted_iota(jnp.int32, (tile, 128), 1)
        gate = jnp.sum(jnp.where(lane == mine, every, 0.0), axis=1, keepdims=True)
        gate_rows[into, :] = jnp.broadcast_to(gate, (tile, 128))

        @pl.loop(0, ff // 256)
        def _(f):
            columns = pl.ds(pl.multiple_of(f * 256, 256), 256)
            g = jnp.dot(tokens[...], gate_w[:, columns], preferred_element_type=jnp.float32)
            u = jnp.dot(tokens[...], up_w[:, columns], preferred_element_type=jnp.float32)
            act[into, columns] = (g / (1.0 + jnp.exp(-g)) * u).astype(jnp.bfloat16)

    for copy in pending:
        copy.wait_send()

    def send_back(q, stage, used):
        bit, runs = plans[q][stage]
        weight = weights[bit]
        started = []
        for start, size in runs:
            @pl.loop(start + weight, start + weight + size, unroll=size <= 4)
            def _(p):
                pair = [
                    total[p, :, q * part + k * piece : q * part + (k + 1) * piece]
                    for k in range(2)
                ]
                rows[q][p, :, :piece] = jnp.concatenate(pair, axis=0).astype(jnp.bfloat16)

            span = pl.ds(start + weight, size)
            copy = pltpu.make_async_remote_copy(
                src_ref=rows[q].at[span, :, pl.ds(0, piece)],
                dst_ref=backs[q].at[span],
                send_sem=send_sem.at[used],
                recv_sem=recv_sem.at[used],
                device_id=partner(bit),
                device_id_type=pl.DeviceIdType.MESH,
            )
            copy.start()
            started.append((start, size, weight, copy))
            used += 1
        return started, used

    def take_back(q, started):
        for start, size, weight, copy in started:
            copy.wait_recv()

            @pl.loop(start, start + size, unroll=size <= 4)
            def _(p):
                both = backs[q][p + weight].astype(jnp.float32)
                for k in range(2):
                    columns = slice(q * part + k * piece, q * part + (k + 1) * piece)
                    total[p, :, columns] += both[8 * k : 8 * k + 8]

    pending = []
    last = len(weights) - 1
    for stage in reversed(range(len(weights))):
        for q in range(4):
            if stage == last:
                @pl.loop(0, count // blocks)
                def _(step):
                    into = pl.ds(pl.multiple_of(step * tile, tile), tile)
                    for k in range(2):
                        columns = slice(q * part + k * piece, q * part + (k + 1) * piece)
                        made = jnp.dot(
                            act[into, :], down_w[:, columns], preferred_element_type=jnp.float32
                        )
                        made = made * gate_rows[into, :1]
                        total[pl.ds(step * blocks, blocks), :, columns] = made.reshape(
                            blocks, 8, piece
                        )
            else:
                take_back(q, arriving[q])
            arriving[q], used = send_back(q, stage, used)
            pending += [entry[3] for entry in arriving[q]]
    for q in range(4):
        take_back(q, arriving[q])
    out_ref[...] = total[0].astype(out_ref.dtype)
    for copy in pending:
        copy.wait_send()


def attention_and_experts(
    queries, key_cache, value_cache, fresh_token_keys, new_values, lengths, hidden_rows, norm_gain, expert_ids, route_scores, gate_weight, up_weight, down_weight
):
    row_count, width = hidden_rows.shape
    node_count = lax.axis_size("node")
    local_count = lax.axis_size("local")
    count = node_count * local_count
    piece = width // 8
    ff = gate_weight.shape[2]
    weights, orders = exchange_orders(node_count, local_count)
    copies = sum(len(runs) for order in orders for _, runs in gather_plan(weights, order))
    tile = min(256, count * row_count)
    vmem = pl.BlockSpec(memory_space=pltpu.VMEM)
    anywhere = pl.BlockSpec(memory_space=pl.ANY)
    rows = count * row_count
    return pl.pallas_call(
        functools.partial(expert_kernel, node_count, local_count),
        out_shape=(
            jax.ShapeDtypeStruct(queries.shape, jnp.bfloat16),
            jax.ShapeDtypeStruct((row_count, width), jnp.bfloat16),
        ),
        in_specs=[vmem] * 3
        + [pl.BlockSpec(memory_space=pltpu.SMEM)]
        + [vmem] * 4
        + [anywhere] * 5,
        out_specs=(vmem, vmem),
        scratch_shapes=[
            pltpu.VMEM((count, 16, piece + 128), jnp.bfloat16),
            *[pltpu.VMEM((count, 16, piece), jnp.bfloat16)] * 7,
            pltpu.VMEM((count, 8, width), jnp.float32),
            pltpu.VMEM((tile, width), jnp.bfloat16),
            pltpu.VMEM((rows, ff), jnp.bfloat16),
            pltpu.VMEM((rows, 128), jnp.float32),
            pltpu.VMEM((width, ff), jnp.bfloat16),
            pltpu.VMEM((width, ff), jnp.bfloat16),
            pltpu.VMEM((ff, width), jnp.bfloat16),
            pltpu.VMEM(key_cache.shape, jnp.bfloat16),
            pltpu.VMEM(value_cache.shape, jnp.bfloat16),
            pltpu.SemaphoreType.DMA((5,)),
            pltpu.SemaphoreType.DMA((2 * copies,)),
            pltpu.SemaphoreType.DMA((2 * copies,)),
        ],
        compiler_params=pltpu.CompilerParams(
            collective_id=0, has_side_effects=True, vmem_limit_bytes=62 * 1024 * 1024
        ),
        cost_estimate=pl.CostEstimate(
            flops=6 * rows * width * ff, bytes_accessed=6 * width * ff, transcendentals=rows * ff
        ),
    )(
        queries, fresh_token_keys, new_values, lengths,
        hidden_rows, norm_gain.reshape(width // 128, 128), expert_ids, route_scores,
        key_cache, value_cache,
        gate_weight, up_weight, down_weight,
    )


def per_device(
    queries,
    key_cache,
    value_cache,
    fresh_token_keys,
    new_values,
    lengths,
    hidden_rows,
    norm_gain,
    expert_ids,
    route_scores,
    gate_weight,
    up_weight,
    down_weight,
):
    context, weighted_expert_total = attention_and_experts(
        queries, key_cache, value_cache, fresh_token_keys, new_values, lengths,
        hidden_rows, norm_gain, expert_ids, route_scores, gate_weight, up_weight, down_weight,
    )
    context = context.reshape(queries.shape[0], queries.shape[1] * queries.shape[2])
    return (context, weighted_expert_total)


def solution(mesh):
    placed = (
        P(("group", "node", "local"), None, None),
        P(("group", "node", "local"), None, None, None),
        P(("group", "node", "local"), None, None, None),
        P(("group", "node", "local"), None, None),
        P(("group", "node", "local"), None, None),
        P(("group", "node", "local")),
        P(("group", "node", "local"), None),
        P(),
        P(("group", "node", "local"), None),
        P(("group", "node", "local"), None),
        P(("node", "local"), None, None),
        P(("node", "local"), None, None),
        P(("node", "local"), None, None),
    )
    return jax.shard_map(
        per_device,
        mesh=mesh,
        in_specs=placed,
        out_specs=(P(("group", "node", "local"), None), P(("group", "node", "local"), None)),
        check_vma=False,
    )
```
